512 devices in a mesh: sta: 64 (over z, x_hi, core), freq: 8 (over y, x_lo).
Axes of the slice: x: 4 (x_hi: 2, x_lo: 2; x = x_hi * 2 + x_lo), y: 4, z: 16, core: 2. Of those that a mesh axis runs over, the one named last changes fastest.
Arguments:
- spectra: bfloat16 [2, 4096, 2048], P(None, 'sta', 'freq'), may hold values from -6 to 6
- station_ok: int32 [4096], P('sta'), may hold values 0 or 1
- pair_mask: int32 [4096, 3, 64], P('sta', None, 'freq'), may hold values 0 or 1
Outputs:
- correlations: float32 [4096, 3, 64, 512], P('sta', None, 'freq')
The draws below stay inside these ranges and needn't reach their ends.
All inputs are finite; a program needn't handle non-finite values. No bound on the sum of `station_ok` or of `pair_mask` on one device may be relied on, other than what follows from the above.
Results may differ from the reference program's by a relative error of at most 0.0054.
Values may be sent and summed in bfloat16 or wider, within the bound.
No kernel may reach another device: no remote copies, remote signals or barrier semaphores. Data moves between devices by JAX's collectives and lax.ppermute only.
A program may use at most 64 MiB of HBM per device.

```python
import math
import jax
import jax.numpy as jnp
from jax import lax

F = 2048
L = 512
H = 4
SHIFTS = 3
SD = 64
S = 4096
N_STA = 64


def plant(array, stream_key, low, high):
    index_at = [jax.random.randint(jax.random.fold_in(stream_key, axis), (), 0, length) for axis, length in enumerate(array.shape)]
    longest = array.shape.index(max(array.shape))
    beside = index_at[:longest] + [(index_at[longest] + 1) % array.shape[longest]] + index_at[longest + 1:]
    return array.at[tuple(index_at)].set(low).at[tuple(beside)].set(high)


def steps_of(key, extent, shards, low, high):
    def one(position, parts):
        steps = jax.random.uniform(jax.random.fold_in(jax.random.fold_in(key, 6), position), (parts,), jnp.float32, low / len(shards), high / len(shards))
        return jnp.repeat(jnp.exp(steps), extent[position] // parts).reshape((-1,) + (1,) * (len(extent) - position - 1))

    level = one(*shards[0])
    for cut in shards[1:]:
        level = level * one(*cut)
    return level


def normal_values(key, dims, scale, most, shards=(), kind=jnp.bfloat16):
    values = scale * jax.random.normal(key, dims, jnp.float32)
    if shards:
        values = values * steps_of(key, dims, shards, -0.22, 0.18)
    return jnp.clip(values, -most, most).astype(kind)


def setup_inputs(seed: int = 0) -> dict:
    splits = jax.random.split(jax.random.key(seed), 4)
    spectra = normal_values(splits[0], (2, S, F), 1.0, 6.0, ((1, 64), (2, 8)))
    station_ok = plant((jax.random.randint(splits[1], (S,), 0, 8) < 7).astype(jnp.int32), jax.random.fold_in(splits[1], 1), 0, 1)
    pair_mask = plant((jax.random.randint(splits[2], (S, SHIFTS, SD), 0, 4) < 3).astype(jnp.int32), jax.random.fold_in(splits[2], 1), 0, 1)
    return {"spectra": spectra, "station_ok": station_ok, "pair_mask": pair_mask}


row_group = 4
epsilon = 1e-06

def whiten(spectra, station_ok):
    values = spectra.astype(jnp.float32)
    weight = station_ok.astype(jnp.float32)[:, None]
    powers = values[0] * values[0] + values[1] * values[1]
    padded = jnp.pad(powers, ((0, 0), (H, H)))
    width = powers.shape[1]
    smooth = jnp.zeros_like(powers)
    for offset in range(2 * H + 1):
        smooth = smooth + padded[:, offset:offset + width]
    smooth = smooth / (2 * H + 1)
    band_mean = lax.optimization_barrier(jnp.sum(powers, axis=1)) / F
    scales = weight / jnp.sqrt(smooth + 0.5 * band_mean[:, None] + epsilon)
    return (values * scales[None]).astype(jnp.bfloat16)

def lag_table(first_lag, count):
    bins = jnp.arange(F, dtype=jnp.int32)
    lag_index = first_lag + jnp.arange(count, dtype=jnp.int32) - L // 2
    phases = bins[:, None] * lag_index[None, :] % (2 * F)
    angles = phases.astype(jnp.float32) * (math.pi / F)
    return jnp.concatenate([jnp.cos(angles), -jnp.sin(angles)], axis=0).astype(jnp.bfloat16)

def cross_lags(own_band, partner, table):
    stations = own_band.shape[1]
    partners = partner.shape[1]
    groups = stations // row_group
    part_real = partner[0].astype(jnp.float32)[None]
    part_imag = partner[1].astype(jnp.float32)[None]
    blocks = own_band.reshape(2, groups, row_group, own_band.shape[2]).transpose(1, 0, 2, 3)

    def group_lags(block):
        own_real = block[0].astype(jnp.float32)[:, None, :]
        own_imag = block[1].astype(jnp.float32)[:, None, :]
        cross_real = own_real * part_real + own_imag * part_imag
        cross_imag = own_imag * part_real - own_real * part_imag
        crossed = jnp.concatenate([cross_real, cross_imag], axis=-1).astype(jnp.bfloat16)
        crossed = crossed.reshape(row_group * partners, crossed.shape[-1])
        lagged = jnp.dot(crossed, table, preferred_element_type=jnp.float32)
        return lagged.reshape(row_group, partners, table.shape[1])
    return lax.map(group_lags, blocks).reshape(stations, partners, table.shape[1])

def reference(spectra, station_ok, pair_mask):
    whitened = whiten(spectra, station_ok)
    blocks = whitened.reshape(2, N_STA, SD, F).transpose(1, 0, 2, 3)
    table = lag_table(0, L)
    results = []
    for offset in range(1, SHIFTS + 1):
        partner = jnp.roll(blocks, -offset, axis=0)
        lagged = lax.map(lambda pair: cross_lags(pair[0], pair[1], table), (blocks, partner))
        results.append(lagged.reshape(S, SD, L))
    stacked = jnp.stack(results, axis=1) * (1.0 / math.sqrt(F))
    return stacked * pair_mask.astype(jnp.float32)[..., None]
```

```python
import math

import jax
import jax.numpy as jnp
import numpy as np
import ml_dtypes
from jax import lax
from jax.experimental import pallas as pl
from jax.experimental.pallas import tpu as pltpu
from jax.sharding import Mesh, PartitionSpec as P

F = 2048
L = 512
H = 4
SHIFTS = 3
HALF = L // 2
LAYER = 4
epsilon = 1e-06
MIB = 1024 * 1024


def tables():
    bins = np.arange(F, dtype=np.int64)
    taus = np.arange(HALF, dtype=np.int64)
    angles = (bins[:, None] * taus[None, :] % (2 * F)).astype(np.float64) * (math.pi / F)
    edge = (bins * HALF % (2 * F)).astype(np.float64) * (math.pi / F)
    bf16 = ml_dtypes.bfloat16
    last = np.stack([np.cos(edge), np.sin(edge)] * 4).astype(bf16).astype(np.float32)
    return np.cos(angles).astype(bf16), (-np.sin(angles)).astype(bf16), last


def whitened(real, imag):
    rows = real.shape[0]
    powers = real * real + imag * imag
    total = jnp.sum(powers, axis=1, keepdims=True)
    padded = jnp.concatenate([powers, jnp.zeros((rows, 128), jnp.float32)], axis=1)
    width = padded.shape[1]
    two = padded + pltpu.roll(padded, 1, 1)
    four = two + pltpu.roll(two, 2, 1)
    eight = four + pltpu.roll(four, 4, 1)
    nine = eight + pltpu.roll(padded, 2 * H, 1)
    smooth = pltpu.roll(nine, width - H, 1)[:, :F]
    scales = lax.rsqrt(smooth * (1.0 / (2 * H + 1)) + total * (0.5 / F) + epsilon)
    return real * scales, imag * scales


def prepare(spectra_hbm, ok_hbm, repeated_ref, source_ref, spectra_ref, ok_ref, valid_ref, turned_ref, sems):
    stations = spectra_ref.shape[1]
    bands, both_rows, _ = source_ref.shape
    partners = both_rows // 2
    loads = [pltpu.make_async_copy(spectra_hbm, spectra_ref, sems.at[0]), pltpu.make_async_copy(ok_hbm, ok_ref, sems.at[1])]
    for load in loads:
        load.start()
    for load in loads:
        load.wait()
    shape = (stations, stations)
    here = lax.broadcasted_iota(jnp.int32, shape, 0) == lax.broadcasted_iota(jnp.int32, shape, 1)
    ok = jnp.where(here, jnp.broadcast_to(ok_ref[...].astype(jnp.float32), shape), 0.0)
    ok = jnp.sum(ok, axis=1, keepdims=True)
    real = spectra_ref[0].astype(jnp.float32) * ok
    imag = spectra_ref[1].astype(jnp.float32) * ok
    valid_ref[0] = real.astype(jnp.bfloat16)
    valid_ref[1] = imag.astype(jnp.bfloat16)
    stores = [pltpu.make_async_copy(valid_ref, repeated_ref.at[q], sems.at[2 + q]) for q in range(bands)]
    for store in stores:
        store.start()
    for q in range(bands):
        rows = slice(q * partners, (q + 1) * partners)
        turned_ref[q] = jnp.concatenate([real[rows], imag[rows]], axis=0).astype(jnp.bfloat16)
    stores.append(pltpu.make_async_copy(turned_ref, source_ref, sems.at[2 + bands]))
    stores[-1].start()
    for store in stores:
        store.wait()


def prepared(spectra, station_ok, bands):
    _, stations, bins = spectra.shape
    turned = (bands, 2 * stations // bands, bins)
    hbm = pl.BlockSpec(memory_space=pl.ANY)
    return pl.pallas_call(
        prepare,
        out_shape=[jax.ShapeDtypeStruct((bands,) + spectra.shape, spectra.dtype),
                   jax.ShapeDtypeStruct(turned, spectra.dtype)],
        in_specs=[hbm] * 2,
        out_specs=[hbm] * 2,
        scratch_shapes=[
            pltpu.VMEM(spectra.shape, spectra.dtype),
            pltpu.VMEM((1, stations), jnp.int32),
            pltpu.VMEM(spectra.shape, spectra.dtype),
            pltpu.VMEM(turned, spectra.dtype),
            pltpu.SemaphoreType.DMA((3 + bands,)),
        ],
        compiler_params=pltpu.CompilerParams(vmem_limit_bytes=60 * MIB),
        cost_estimate=pl.CostEstimate(flops=spectra.size, bytes_accessed=2 * 10 * spectra.size, transcendentals=0),
    )(spectra, station_ok.reshape(1, stations))


def choose(place_ref, source_ref, above_ref, sent_ref):
    bands = source_ref.shape[0]
    for other in range(LAYER):
        to = sent_ref.at[other * bands:(other + 1) * bands]

        @pl.when(other < place_ref[0])
        def _():
            to[...] = source_ref[...]

        @pl.when(other >= place_ref[0])
        def _():
            to[...] = above_ref[...]


def chosen(place, source, above):
    vmem = pl.BlockSpec(memory_space=pltpu.VMEM)
    return pl.pallas_call(
        choose,
        out_shape=jax.ShapeDtypeStruct((LAYER * source.shape[0],) + source.shape[1:], source.dtype),
        in_specs=[pl.BlockSpec(memory_space=pltpu.SMEM)] + [vmem] * 2,
        out_specs=vmem,
        compiler_params=pltpu.CompilerParams(vmem_limit_bytes=8 * MIB),
        cost_estimate=pl.CostEstimate(flops=0, bytes_accessed=2 * 6 * source.size, transcendentals=0),
    )(place, source, above)


def whiten(own_ref, cos_from, sin_from, last_from, real_ref, imag_ref, cos_ref, sin_ref, last_ref, sems):
    bands = own_ref.shape[0]
    pairs = ((cos_from, cos_ref), (sin_from, sin_ref), (last_from, last_ref))
    loads = [pltpu.make_async_copy(table, to, sems.at[i]) for i, (table, to) in enumerate(pairs)]
    for load in loads:
        load.start()

    def some(group, carry):
        at = pl.ds(pl.multiple_of(group * 16, 16), 16)
        real = jnp.concatenate([own_ref[q, 0, at, :] for q in range(bands)], axis=1)
        imag = jnp.concatenate([own_ref[q, 1, at, :] for q in range(bands)], axis=1)
        real, imag = whitened(real.astype(jnp.float32), imag.astype(jnp.float32))
        real_ref[at, :] = real.astype(jnp.bfloat16)
        imag_ref[at, :] = imag.astype(jnp.bfloat16)
        return carry

    lax.fori_loop(0, real_ref.shape[0] // 16, some, 0)
    for load in loads:
        load.wait()


def whitened_block(own):
    stations = own.shape[2]
    given = [jnp.asarray(table) for table in tables()]
    vmem = pl.BlockSpec(memory_space=pltpu.VMEM)
    return pl.pallas_call(
        whiten,
        out_shape=[jax.ShapeDtypeStruct((stations, F), jnp.bfloat16)] * 2
        + [jax.ShapeDtypeStruct(table.shape, table.dtype) for table in given],
        in_specs=[vmem] + [pl.BlockSpec(memory_space=pl.ANY)] * 3,
        out_specs=[vmem] * 5,
        scratch_shapes=[pltpu.SemaphoreType.DMA((3,))],
        compiler_params=pltpu.CompilerParams(vmem_limit_bytes=8 * MIB),
        cost_estimate=pl.CostEstimate(flops=30 * stations * F, bytes_accessed=8 * stations * F, transcendentals=stations * F),
    )(own, *given)


def correlate(place_ref, own_real, own_imag, cos_ref, sin_ref, last_ref, part_ref, mask_ref, out_ref,
              part_real, part_imag, turned, cross_real, cross_imag, lags, sems):
    stations = own_real.shape[0]
    bands = part_ref.shape[0] // LAYER
    partners = part_ref.shape[1] // 2
    last_cos = last_ref[0:1, :]
    last_sin = last_ref[1:2, :]
    for k in range(SHIFTS):
        first = lax.rem(place_ref[0] + (k + 1), LAYER) * bands
        both = jnp.concatenate([part_ref[first + q] for q in range(bands)], axis=1).astype(jnp.float32)
        real, imag = whitened(both[:partners], both[partners:])
        real = real.astype(jnp.bfloat16).astype(jnp.float32)
        imag = imag.astype(jnp.bfloat16).astype(jnp.float32)
        part_real[k * partners:(k + 1) * partners, :] = real
        part_imag[k * partners:(k + 1) * partners, :] = imag
        turned[0, k * partners:(k + 1) * partners, :] = real * last_cos - imag * last_sin
        turned[1, k * partners:(k + 1) * partners, :] = imag * last_cos + real * last_sin

    edge = jnp.zeros((stations, SHIFTS * partners), jnp.float32)
    for c, own in ((0, own_real), (1, own_imag)):
        high = turned[c].astype(jnp.bfloat16)
        low = (turned[c] - high.astype(jnp.float32)).astype(jnp.bfloat16)
        for part in (high, low):
            edge = edge + lax.dot_general(own[...], part, (((1,), (1,)), ((), ())),
                                          preferred_element_type=jnp.float32)
    edge = edge * mask_ref[...]

    def finished(k, q):
        rows = lags.at[k, q].reshape(stations, partners, 128)
        return pltpu.make_async_copy(rows, out_ref.at[:, k, :, pl.ds(q * 128, 128)], sems.at[k, q])

    lane = lax.broadcasted_iota(jnp.int32, (stations, 128), 1)
    mirror = lax.rem(128 - lane, 128)
    for k in range(SHIFTS):
        def cross(j, carry):
            row = k * partners + j
            at = pl.ds(pl.multiple_of(j * stations, 16), stations)
            other_real = jnp.broadcast_to(part_real[pl.ds(row, 1), :], (16, F)).astype(jnp.bfloat16)
            other_imag = jnp.broadcast_to(part_imag[pl.ds(row, 1), :], (16, F)).astype(jnp.bfloat16)
            for g in range(stations // 16):
                real = own_real[g * 16:(g + 1) * 16, :]
                imag = own_imag[g * 16:(g + 1) * 16, :]
                at = pl.ds(pl.multiple_of(j * stations + g * 16, 16), 16)
                cross_real[at, :] = real * other_real + imag * other_imag
                cross_imag[at, :] = imag * other_real - real * other_imag
            return carry

        lax.fori_loop(0, partners, cross, 0)
        even = jnp.dot(cross_real[...], cos_ref[...], preferred_element_type=jnp.float32)
        odd = jnp.dot(cross_imag[...], sin_ref[...], preferred_element_type=jnp.float32)
        for j in range(partners):
            column = k * partners + j
            weight = mask_ref[:, column:column + 1]
            c = even[j * stations:(j + 1) * stations, :] * weight
            s = odd[j * stations:(j + 1) * stations, :] * weight
            up = c + s
            down = c - s
            near, far = down[:, :128], down[:, 128:]
            ends = jnp.broadcast_to(edge[:, column:column + 1], (stations, 128))
            first = jnp.take_along_axis(jnp.where(lane == 0, ends, far), mirror, axis=1)
            second = jnp.take_along_axis(jnp.where(lane == 0, far, near), mirror, axis=1)
            at = pl.ds(j, stations, stride=partners)
            for q, piece in enumerate((first, second, up[:, :128], up[:, 128:])):
                lags[k, q, at, :] = piece
        for q in range(4):
            finished(k, q).start()
    for k in range(SHIFTS):
        for q in range(4):
            finished(k, q).wait()


def correlations_of(place, own, parts, mask):
    stations = own[0].shape[0]
    partners = parts.shape[1] // 2
    vmem = pl.BlockSpec(memory_space=pltpu.VMEM)
    return pl.pallas_call(
        correlate,
        out_shape=jax.ShapeDtypeStruct((stations, SHIFTS, partners, L), jnp.float32),
        in_specs=[pl.BlockSpec(memory_space=pltpu.SMEM)] + [vmem] * 7,
        out_specs=pl.BlockSpec(memory_space=pl.ANY),
        scratch_shapes=[
            pltpu.VMEM((SHIFTS * partners, F), jnp.float32),
            pltpu.VMEM((SHIFTS * partners, F), jnp.float32),
            pltpu.VMEM((2, SHIFTS * partners, F), jnp.float32),
            pltpu.VMEM((stations * partners, F), jnp.bfloat16),
            pltpu.VMEM((stations * partners, F), jnp.bfloat16),
            pltpu.VMEM((SHIFTS, L // 128, stations * partners, 128), jnp.float32),
            pltpu.SemaphoreType.DMA((SHIFTS, L // 128)),
        ],
        compiler_params=pltpu.CompilerParams(vmem_limit_bytes=24 * MIB),
        cost_estimate=pl.CostEstimate(
            flops=2 * SHIFTS * stations * partners * 2 * F * HALF,
            bytes_accessed=SHIFTS * stations * partners * L * 4,
            transcendentals=0),
    )(place, *own, parts, mask)


def shards(spectra, station_ok, pair_mask):
    bands, layers = lax.axis_size("freq"), lax.axis_size("layer")
    stations = spectra.shape[1]
    partners = stations // bands
    repeated, source = prepared(spectra, station_ok, bands)
    own = lax.all_to_all(repeated, "freq", 0, 0)
    above = lax.ppermute(source, "layer", [((i + 1) % layers, i) for i in range(layers)])
    above, own = lax.optimization_barrier((above, own))
    place = lax.axis_index("block").reshape(1)
    parts = lax.all_to_all(chosen(place, source, above), ("block", "freq"), 0, 0)
    mask = pair_mask.reshape(stations, SHIFTS * partners).astype(jnp.float32) * (1.0 / math.sqrt(F))
    return correlations_of(place, whitened_block(own), parts, mask)


def solution(mesh):
    blocks, bands = mesh.shape["sta"], mesh.shape["freq"]
    inner = Mesh(mesh.devices.reshape(blocks // LAYER, LAYER, bands), ("layer", "block", "freq"))
    sta = ("layer", "block")
    return jax.shard_map(
        shards,
        mesh=inner,
        in_specs=(P(None, sta, "freq"), P(sta), P(sta, None, "freq")),
        out_specs=P(sta, None, "freq", None),
        check_vma=False,
    )
```

```python
import math

import jax
import jax.numpy as jnp
import numpy as np
import ml_dtypes
from jax import lax
from jax.experimental import pallas as pl
from jax.experimental.pallas import tpu as pltpu
from jax.sharding import Mesh, PartitionSpec as P

F = 2048
L = 512
H = 4
SHIFTS = 3
HALF = L // 2
LAYER = 4
epsilon = 1e-06
MIB = 1024 * 1024
GROUP = 4


def tables():
    bins = np.arange(F, dtype=np.int64)
    taus = np.arange(HALF, dtype=np.int64)
    angles = (bins[:, None] * taus[None, :] % (2 * F)).astype(np.float64) * (math.pi / F)
    return [half.astype(ml_dtypes.bfloat16) for half in (np.cos(angles), -np.sin(angles))]


def edge_rows():
    turn = 2 * F // HALF
    lane = lax.broadcasted_iota(jnp.int32, (8, 128), 1) % turn
    cos = sin = jnp.zeros((8, 128), jnp.float32)
    for r in range(turn):
        angle = 2 * math.pi * r / turn
        values = np.array([math.cos(angle), math.sin(angle)]).astype(ml_dtypes.bfloat16)
        cos = jnp.where(lane == r, float(values[0]), cos)
        sin = jnp.where(lane == r, float(values[1]), sin)
    return jnp.concatenate([cos] * (F // 128), axis=1), jnp.concatenate([sin] * (F // 128), axis=1)


def whitened(real, imag):
    rows = real.shape[0]
    powers = real * real + imag * imag
    total = jnp.sum(powers, axis=1, keepdims=True)
    padded = jnp.concatenate([powers, jnp.zeros((rows, 128), jnp.float32)], axis=1)
    width = padded.shape[1]
    two = padded + pltpu.roll(padded, 1, 1)
    four = two + pltpu.roll(two, 2, 1)
    eight = four + pltpu.roll(four, 4, 1)
    nine = eight + pltpu.roll(padded, 2 * H, 1)
    smooth = pltpu.roll(nine, width - H, 1)[:, :F]
    scales = lax.rsqrt(smooth * (1.0 / (2 * H + 1)) + total * (0.5 / F) + epsilon)
    return real * scales, imag * scales


def prepare(spectra_hbm, ok_hbm, repeated_ref, source_ref, spectra_ref, ok_ref, valid_ref, turned_ref, sems):
    stations = spectra_ref.shape[1]
    bands = source_ref.shape[0]
    loads = [pltpu.make_async_copy(spectra_hbm, spectra_ref, sems.at[0]), pltpu.make_async_copy(ok_hbm, ok_ref, sems.at[1])]
    for load in loads:
        load.start()
    for load in loads:
        load.wait()
    shape = (stations, stations)
    here = lax.broadcasted_iota(jnp.int32, shape, 0) == lax.broadcasted_iota(jnp.int32, shape, 1)
    ok = jnp.where(here, jnp.broadcast_to(ok_ref[...].astype(jnp.float32), shape), 0.0)
    ok = jnp.sum(ok, axis=1, keepdims=True)
    real = spectra_ref[0].astype(jnp.float32) * ok
    imag = spectra_ref[1].astype(jnp.float32) * ok
    valid_ref[0] = real.astype(jnp.bfloat16)
    valid_ref[1] = imag.astype(jnp.bfloat16)
    stores = [pltpu.make_async_copy(valid_ref, repeated_ref.at[q], sems.at[2 + q]) for q in range(bands)]
    for store in stores:
        store.start()
    turn(real, imag, turned_ref)
    stores.append(pltpu.make_async_copy(turned_ref, source_ref, sems.at[2 + bands]))
    stores[-1].start()
    for store in stores:
        store.wait()


def prepared(spectra, station_ok, bands):
    _, stations, bins = spectra.shape
    turned = (bands, 2 * stations // bands, bins)
    hbm = pl.BlockSpec(memory_space=pl.ANY)
    return pl.pallas_call(
        prepare,
        out_shape=[jax.ShapeDtypeStruct((bands,) + spectra.shape, spectra.dtype),
                   jax.ShapeDtypeStruct(turned, spectra.dtype)],
        in_specs=[hbm] * 2,
        out_specs=[hbm] * 2,
        scratch_shapes=[
            pltpu.VMEM(spectra.shape, spectra.dtype),
            pltpu.VMEM((1, stations), jnp.int32),
            pltpu.VMEM(spectra.shape, spectra.dtype),
            pltpu.VMEM(turned, spectra.dtype),
            pltpu.SemaphoreType.DMA((3 + bands,)),
        ],
        compiler_params=pltpu.CompilerParams(vmem_limit_bytes=60 * MIB),
        cost_estimate=pl.CostEstimate(flops=spectra.size, bytes_accessed=2 * 10 * spectra.size, transcendentals=0),
    )(spectra, station_ok.reshape(1, stations))


def turn(real, imag, turned_ref):
    bands, both_rows, _ = turned_ref.shape
    partners = both_rows // 2
    for q in range(bands):
        rows = slice(q * partners, (q + 1) * partners)
        turned_ref[q] = jnp.concatenate([real[rows], imag[rows]], axis=0).astype(jnp.bfloat16)


def choose(place_ref, source_ref, above_ref, sent_ref):
    bands = source_ref.shape[0]
    for other in range(LAYER):
        to = sent_ref.at[other * bands:(other + 1) * bands]

        @pl.when(other < place_ref[0])
        def _():
            to[...] = source_ref[...]

        @pl.when(other >= place_ref[0])
        def _():
            to[...] = above_ref[...]


def chosen(place, source, above):
    vmem = pl.BlockSpec(memory_space=pltpu.VMEM)
    return pl.pallas_call(
        choose,
        out_shape=jax.ShapeDtypeStruct((LAYER * source.shape[0],) + source.shape[1:], source.dtype),
        in_specs=[pl.BlockSpec(memory_space=pltpu.SMEM)] + [vmem] * 2,
        out_specs=vmem,
        compiler_params=pltpu.CompilerParams(vmem_limit_bytes=8 * MIB),
        cost_estimate=pl.CostEstimate(flops=0, bytes_accessed=2 * 6 * source.size, transcendentals=0),
    )(place, source, above)


def whiten(own_ref, cos_from, sin_from, real_ref, imag_ref, cos_ref, sin_ref, sems):
    bands = own_ref.shape[0]
    pairs = ((cos_from, cos_ref), (sin_from, sin_ref))
    loads = [pltpu.make_async_copy(table, to, sems.at[i]) for i, (table, to) in enumerate(pairs)]
    for load in loads:
        load.start()

    def some(group, carry):
        at = pl.ds(pl.multiple_of(group * 16, 16), 16)
        real = jnp.concatenate([own_ref[q, 0, at, :] for q in range(bands)], axis=1)
        imag = jnp.concatenate([own_ref[q, 1, at, :] for q in range(bands)], axis=1)
        real, imag = whitened(real.astype(jnp.float32), imag.astype(jnp.float32))
        real_ref[at, :] = real.astype(jnp.bfloat16)
        imag_ref[at, :] = imag.astype(jnp.bfloat16)
        return carry

    lax.fori_loop(0, real_ref.shape[0] // 16, some, 0)
    for load in loads:
        load.wait()


def whitened_block(own):
    stations = own.shape[2]
    given = [jnp.asarray(table) for table in tables()]
    vmem = pl.BlockSpec(memory_space=pltpu.VMEM)
    return pl.pallas_call(
        whiten,
        out_shape=[jax.ShapeDtypeStruct((stations, F), jnp.bfloat16)] * 2
        + [jax.ShapeDtypeStruct(table.shape, table.dtype) for table in given],
        in_specs=[vmem] + [pl.BlockSpec(memory_space=pl.ANY)] * 2,
        out_specs=[vmem] * 4,
        scratch_shapes=[pltpu.SemaphoreType.DMA((2,))],
        compiler_params=pltpu.CompilerParams(vmem_limit_bytes=8 * MIB),
        cost_estimate=pl.CostEstimate(flops=30 * stations * F, bytes_accessed=8 * stations * F, transcendentals=stations * F),
    )(own, *given)


def correlate(place_ref, own_real, own_imag, cos_ref, sin_ref, part_ref, mask_ref, out_ref,
              others, cross, lags, sems):
    stations = own_real.shape[0]
    bands = part_ref.shape[0] // LAYER
    partners = part_ref.shape[1] // 2
    last_cos, last_sin = edge_rows()
    lane = lax.broadcasted_iota(jnp.int32, (stations, 128), 1)
    mirror = lax.rem(128 - lane, 128)
    parts_per_shift = partners // GROUP
    steps = [(k, g) for k in range(SHIFTS) for g in range(parts_per_shift)]

    def whiten_part(k):
        first = lax.rem(place_ref[0] + (k + 1), LAYER) * bands
        both = jnp.concatenate([part_ref[first + q] for q in range(bands)], axis=1).astype(jnp.float32)
        real, imag = whitened(both[:partners], both[partners:])
        real = real.astype(jnp.bfloat16).astype(jnp.float32)
        imag = imag.astype(jnp.bfloat16).astype(jnp.float32)
        others[k, 0] = real
        others[k, 1] = imag
        edge = jnp.zeros((stations, partners), jnp.float32)
        for own, turned in ((own_real, real * last_cos - imag * last_sin), (own_imag, imag * last_cos + real * last_sin)):
            edge = edge + lax.dot_general(own[...], turned.astype(jnp.bfloat16), (((1,), (1,)), ((), ())),
                                          preferred_element_type=jnp.float32)
        return edge * mask_ref[:, k * partners:(k + 1) * partners]

    def form(n):
        k, g = steps[n]
        for p in range(GROUP):
            j = g * GROUP + p
            other_real = jnp.broadcast_to(others[k, 0, j:j + 1, :], (16, F)).astype(jnp.bfloat16)
            other_imag = jnp.broadcast_to(others[k, 1, j:j + 1, :], (16, F)).astype(jnp.bfloat16)
            for i in range(stations // 16):
                real = own_real[i * 16:(i + 1) * 16, :]
                imag = own_imag[i * 16:(i + 1) * 16, :]
                at = slice(p * stations + i * 16, p * stations + (i + 1) * 16)
                cross[n % 2, 0, at, :] = real * other_real + imag * other_imag
                cross[n % 2, 1, at, :] = imag * other_real - real * other_imag

    def product(n):
        return (jnp.dot(cross[n % 2, 0], cos_ref[...], preferred_element_type=jnp.float32),
                jnp.dot(cross[n % 2, 1], sin_ref[...], preferred_element_type=jnp.float32))

    def finished(k, q):
        rows = lags.at[k, q].reshape(stations, partners, 128)
        return pltpu.make_async_copy(rows, out_ref.at[:, k, :, pl.ds(q * 128, 128)], sems.at[k, q])

    def finish(n, pair, edge):
        k, g = steps[n]
        even, odd = pair
        down = []
        for half in (0, 1):
            for p in range(GROUP):
                j = g * GROUP + p
                weight = mask_ref[:, k * partners + j:k * partners + j + 1]
                rows = slice(p * stations, (p + 1) * stations)
                c = even[rows, half * 128:(half + 1) * 128] * weight
                s = odd[rows, half * 128:(half + 1) * 128] * weight
                lags[k, 2 + half, pl.ds(j, stations, stride=partners), :] = c + s
                down.append(c - s)
            if g == parts_per_shift - 1:
                finished(k, 2 + half).start()
        for half in (0, 1):
            for p in range(GROUP):
                j = g * GROUP + p
                near, far = down[p], down[GROUP + p]
                if half == 0:
                    ends = jnp.broadcast_to(edge[:, j:j + 1], (stations, 128))
                    piece = jnp.where(lane == 0, ends, far)
                else:
                    piece = jnp.where(lane == 0, far, near)
                lags[k, half, pl.ds(j, stations, stride=partners), :] = jnp.take_along_axis(piece, mirror, axis=1)
            if g == parts_per_shift - 1:
                finished(k, half).start()

    edges = [whiten_part(0)]
    form(0)
    before = None
    for n in range(len(steps)):
        pair = product(n)
        if n + 1 < len(steps):
            if steps[n + 1][1] == 0:
                edges.append(whiten_part(steps[n + 1][0]))
            form(n + 1)
        if before is not None:
            finish(n - 1, before, edges[steps[n - 1][0]])
        before = pair
    finish(len(steps) - 1, before, edges[-1])
    for k in range(SHIFTS):
        for q in range(4):
            finished(k, q).wait()


def correlations_of(place, own, parts, mask):
    stations = own[0].shape[0]
    partners = parts.shape[1] // 2
    vmem = pl.BlockSpec(memory_space=pltpu.VMEM)
    return pl.pallas_call(
        correlate,
        out_shape=jax.ShapeDtypeStruct((stations, SHIFTS, partners, L), jnp.float32),
        in_specs=[pl.BlockSpec(memory_space=pltpu.SMEM)] + [vmem] * 6,
        out_specs=pl.BlockSpec(memory_space=pl.ANY),
        scratch_shapes=[
            pltpu.VMEM((SHIFTS, 2, partners, F), jnp.float32),
            pltpu.VMEM((2, 2, GROUP * stations, F), jnp.bfloat16),
            pltpu.VMEM((SHIFTS, L // 128, stations * partners, 128), jnp.float32),
            pltpu.SemaphoreType.DMA((SHIFTS, L // 128)),
        ],
        compiler_params=pltpu.CompilerParams(vmem_limit_bytes=24 * MIB),
        cost_estimate=pl.CostEstimate(
            flops=2 * SHIFTS * stations * partners * 2 * F * HALF,
            bytes_accessed=SHIFTS * stations * partners * L * 4,
            transcendentals=0),
    )(place, *own, parts, mask)


def shards(spectra, station_ok, pair_mask):
    bands, layers = lax.axis_size("freq"), lax.axis_size("layer")
    stations = spectra.shape[1]
    partners = stations // bands
    repeated, source = prepared(spectra, station_ok, bands)
    own = lax.all_to_all(repeated, "freq", 0, 0)
    above = lax.ppermute(source, "layer", [((i + 1) % layers, i) for i in range(layers)])
    above, own = lax.optimization_barrier((above, own))
    place = lax.axis_index("block").reshape(1)
    parts = lax.all_to_all(chosen(place, source, above), ("block", "freq"), 0, 0)
    mask = pair_mask.reshape(stations, SHIFTS * partners).astype(jnp.float32) * (1.0 / math.sqrt(F))
    return correlations_of(place, whitened_block(own), parts, mask)


def solution(mesh):
    blocks, bands = mesh.shape["sta"], mesh.shape["freq"]
    inner = Mesh(mesh.devices.reshape(blocks // LAYER, LAYER, bands), ("layer", "block", "freq"))
    sta = ("layer", "block")
    return jax.shard_map(
        shards,
        mesh=inner,
        in_specs=(P(None, sta, "freq"), P(sta), P(sta, None, "freq")),
        out_specs=P(sta, None, "freq", None),
        check_vma=False,
    )
```

```python
import math

import jax
import jax.numpy as jnp
import numpy as np
import ml_dtypes
from jax import lax
from jax.experimental import pallas as pl
from jax.experimental.pallas import tpu as pltpu
from jax.sharding import Mesh, PartitionSpec as P

F = 2048
L = 512
H = 4
SHIFTS = 3
HALF = L // 2
LAYER = 4
epsilon = 1e-06
MIB = 1024 * 1024
ROWS = 32


def tables():
    bins = np.arange(F, dtype=np.int64)
    taus = np.arange(HALF, dtype=np.int64)
    angles = (bins[:, None] * taus[None, :] % (2 * F)).astype(np.float64) * (math.pi / F)
    return [half.astype(ml_dtypes.bfloat16) for half in (np.cos(angles), -np.sin(angles))]


def edge_rows():
    turn = 2 * F // HALF
    lane = lax.broadcasted_iota(jnp.int32, (8, 128), 1) % turn
    cos = sin = jnp.zeros((8, 128), jnp.float32)
    for r in range(turn):
        angle = 2 * math.pi * r / turn
        values = np.array([math.cos(angle), math.sin(angle)]).astype(ml_dtypes.bfloat16)
        cos = jnp.where(lane == r, float(values[0]), cos)
        sin = jnp.where(lane == r, float(values[1]), sin)
    return jnp.concatenate([cos] * (F // 128), axis=1), jnp.concatenate([sin] * (F // 128), axis=1)


def whitened(real, imag):
    rows = real.shape[0]
    powers = real * real + imag * imag
    total = jnp.sum(powers, axis=1, keepdims=True)
    padded = jnp.concatenate([powers, jnp.zeros((rows, 128), jnp.float32)], axis=1)
    width = padded.shape[1]
    two = padded + pltpu.roll(padded, 1, 1)
    four = two + pltpu.roll(two, 2, 1)
    eight = four + pltpu.roll(four, 4, 1)
    nine = eight + pltpu.roll(padded, 2 * H, 1)
    smooth = pltpu.roll(nine, width - H, 1)[:, :F]
    scales = lax.rsqrt(smooth * (1.0 / (2 * H + 1)) + total * (0.5 / F) + epsilon)
    return real * scales, imag * scales


def prepare(spectra_hbm, ok_hbm, repeated_ref, source_ref, spectra_ref, ok_ref, valid_ref, turned_ref, sems):
    stations = spectra_ref.shape[1]
    bands = source_ref.shape[0]
    loads = [pltpu.make_async_copy(spectra_hbm, spectra_ref, sems.at[0]), pltpu.make_async_copy(ok_hbm, ok_ref, sems.at[1])]
    for load in loads:
        load.start()
    for load in loads:
        load.wait()
    shape = (stations, stations)
    here = lax.broadcasted_iota(jnp.int32, shape, 0) == lax.broadcasted_iota(jnp.int32, shape, 1)
    ok = jnp.where(here, jnp.broadcast_to(ok_ref[...].astype(jnp.float32), shape), 0.0)
    ok = jnp.sum(ok, axis=1, keepdims=True)
    real = spectra_ref[0].astype(jnp.float32) * ok
    imag = spectra_ref[1].astype(jnp.float32) * ok
    valid_ref[0] = real.astype(jnp.bfloat16)
    valid_ref[1] = imag.astype(jnp.bfloat16)
    stores = [pltpu.make_async_copy(valid_ref, repeated_ref.at[q], sems.at[2 + q]) for q in range(bands)]
    for store in stores:
        store.start()
    turn(real, imag, turned_ref)
    stores.append(pltpu.make_async_copy(turned_ref, source_ref, sems.at[2 + bands]))
    stores[-1].start()
    for store in stores:
        store.wait()


def prepared(spectra, station_ok, bands):
    _, stations, bins = spectra.shape
    turned = (bands, 2 * stations // bands, bins)
    hbm = pl.BlockSpec(memory_space=pl.ANY)
    return pl.pallas_call(
        prepare,
        out_shape=[jax.ShapeDtypeStruct((bands,) + spectra.shape, spectra.dtype),
                   jax.ShapeDtypeStruct(turned, spectra.dtype)],
        in_specs=[hbm] * 2,
        out_specs=[hbm] * 2,
        scratch_shapes=[
            pltpu.VMEM(spectra.shape, spectra.dtype),
            pltpu.VMEM((1, stations), jnp.int32),
            pltpu.VMEM(spectra.shape, spectra.dtype),
            pltpu.VMEM(turned, spectra.dtype),
            pltpu.SemaphoreType.DMA((3 + bands,)),
        ],
        compiler_params=pltpu.CompilerParams(vmem_limit_bytes=60 * MIB),
        cost_estimate=pl.CostEstimate(flops=spectra.size, bytes_accessed=2 * 10 * spectra.size, transcendentals=0),
    )(spectra, station_ok.reshape(1, stations))


def turn(real, imag, turned_ref):
    bands, both_rows, _ = turned_ref.shape
    partners = both_rows // 2
    for q in range(bands):
        rows = slice(q * partners, (q + 1) * partners)
        turned_ref[q] = jnp.concatenate([real[rows], imag[rows]], axis=0).astype(jnp.bfloat16)


def stage(source_ref, staged_ref):
    staged_ref[...] = source_ref[...]


def staged(source):
    vmem = pl.BlockSpec(memory_space=pltpu.VMEM)
    return pl.pallas_call(
        stage,
        out_shape=jax.ShapeDtypeStruct(source.shape, source.dtype),
        in_specs=[vmem],
        out_specs=vmem,
        compiler_params=pltpu.CompilerParams(vmem_limit_bytes=8 * MIB),
        cost_estimate=pl.CostEstimate(flops=0, bytes_accessed=4 * source.size, transcendentals=0),
    )(source)


def choose(place_ref, source_ref, above_ref, sent_ref):
    bands = source_ref.shape[0]
    for other in range(LAYER):
        to = sent_ref.at[other * bands:(other + 1) * bands]

        @pl.when(other < place_ref[0])
        def _():
            to[...] = source_ref[...]

        @pl.when(other >= place_ref[0])
        def _():
            to[...] = above_ref[...]


def chosen(place, source, above):
    vmem = pl.BlockSpec(memory_space=pltpu.VMEM)
    return pl.pallas_call(
        choose,
        out_shape=jax.ShapeDtypeStruct((LAYER * source.shape[0],) + source.shape[1:], source.dtype),
        in_specs=[pl.BlockSpec(memory_space=pltpu.SMEM)] + [vmem] * 2,
        out_specs=vmem,
        compiler_params=pltpu.CompilerParams(vmem_limit_bytes=8 * MIB),
        cost_estimate=pl.CostEstimate(flops=0, bytes_accessed=2 * 6 * source.size, transcendentals=0),
    )(place, source, above)


def whiten(own_ref, cos_from, sin_from, real_ref, imag_ref, cos_ref, sin_ref, sems):
    bands = own_ref.shape[0]
    pairs = ((cos_from, cos_ref), (sin_from, sin_ref))
    loads = [pltpu.make_async_copy(table, to, sems.at[i]) for i, (table, to) in enumerate(pairs)]
    for load in loads:
        load.start()

    def some(group, carry):
        at = pl.ds(pl.multiple_of(group * 16, 16), 16)
        real = jnp.concatenate([own_ref[q, 0, at, :] for q in range(bands)], axis=1)
        imag = jnp.concatenate([own_ref[q, 1, at, :] for q in range(bands)], axis=1)
        real, imag = whitened(real.astype(jnp.float32), imag.astype(jnp.float32))
        real_ref[at, :] = real.astype(jnp.bfloat16)
        imag_ref[at, :] = imag.astype(jnp.bfloat16)
        return carry

    lax.fori_loop(0, real_ref.shape[0] // 16, some, 0)
    for load in loads:
        load.wait()


def whitened_block(own):
    stations = own.shape[2]
    given = [jnp.asarray(table) for table in tables()]
    vmem = pl.BlockSpec(memory_space=pltpu.VMEM)
    return pl.pallas_call(
        whiten,
        out_shape=[jax.ShapeDtypeStruct((stations, F), jnp.bfloat16)] * 2
        + [jax.ShapeDtypeStruct(table.shape, table.dtype) for table in given],
        in_specs=[vmem] + [pl.BlockSpec(memory_space=pl.ANY)] * 2,
        out_specs=[vmem] * 4,
        scratch_shapes=[pltpu.SemaphoreType.DMA((2,))],
        compiler_params=pltpu.CompilerParams(vmem_limit_bytes=8 * MIB),
        cost_estimate=pl.CostEstimate(flops=30 * stations * F, bytes_accessed=8 * stations * F, transcendentals=stations * F),
    )(own, *given)


def correlate(place_ref, own_real, own_imag, cos_ref, sin_ref, part_ref, mask_ref, out_ref,
              others, cross, lags, sems):
    stations = own_real.shape[0]
    bands = part_ref.shape[0] // LAYER
    partners = part_ref.shape[1] // 2
    last_cos, last_sin = edge_rows()
    lane = lax.broadcasted_iota(jnp.int32, (ROWS, 128), 1)
    mirror = lax.rem(128 - lane, 128)
    steps = [(k, slice(i, i + ROWS)) for k in range(SHIFTS) for i in range(0, stations, ROWS)]

    def whiten_part(k):
        first = lax.rem(place_ref[0] + (k + 1), LAYER) * bands
        both = jnp.concatenate([part_ref[first + q] for q in range(bands)], axis=1).astype(jnp.float32)
        real, imag = whitened(both[:partners], both[partners:])
        real = real.astype(jnp.bfloat16).astype(jnp.float32)
        imag = imag.astype(jnp.bfloat16).astype(jnp.float32)
        for j in range(partners):
            others[k % 2, 0, j] = jnp.broadcast_to(real[j:j + 1], (16, F)).astype(jnp.bfloat16)
            others[k % 2, 1, j] = jnp.broadcast_to(imag[j:j + 1], (16, F)).astype(jnp.bfloat16)
        edge = jnp.zeros((stations, partners), jnp.float32)
        for own, turned in ((own_real, real * last_cos - imag * last_sin), (own_imag, imag * last_cos + real * last_sin)):
            edge = edge + lax.dot_general(own[...], turned.astype(jnp.bfloat16), (((1,), (1,)), ((), ())),
                                          preferred_element_type=jnp.float32)
        return edge * mask_ref[:, k * partners:(k + 1) * partners]

    def form(n):
        k, rows = steps[n]
        for j in range(partners):
            for i in range(0, ROWS, 16):
                real = own_real[rows.start + i:rows.start + i + 16, :]
                imag = own_imag[rows.start + i:rows.start + i + 16, :]
                other_real, other_imag = others[k % 2, 0, j], others[k % 2, 1, j]
                at = slice(j * ROWS + i, j * ROWS + i + 16)
                cross[n % 2, 0, at, :] = real * other_real + imag * other_imag
                cross[n % 2, 1, at, :] = imag * other_real - real * other_imag

    def product(n):
        return (jnp.dot(cross[n % 2, 0], cos_ref[...], preferred_element_type=jnp.float32),
                jnp.dot(cross[n % 2, 1], sin_ref[...], preferred_element_type=jnp.float32))

    def finished(n, q):
        k, rows = steps[n]
        ready = lags.at[n, q].reshape(ROWS, partners, 128)
        return pltpu.make_async_copy(ready, out_ref.at[pl.ds(rows.start, ROWS), k, :, pl.ds(q * 128, 128)], sems.at[n, q])

    def finish(n, pair, edge):
        k, rows = steps[n]
        even, odd = pair
        down = []
        for half in (0, 1):
            for j in range(partners):
                weight = mask_ref[rows, k * partners + j:k * partners + j + 1]
                at = slice(j * ROWS, (j + 1) * ROWS)
                c = even[at, half * 128:(half + 1) * 128] * weight
                s = odd[at, half * 128:(half + 1) * 128] * weight
                lags[n, 2 + half, pl.ds(j, ROWS, stride=partners), :] = c + s
                down.append(c - s)
        for half in (0, 1):
            for j in range(partners):
                near, far = down[j], down[partners + j]
                if half == 0:
                    ends = jnp.broadcast_to(edge[rows, j:j + 1], (ROWS, 128))
                    piece = jnp.where(lane == 0, ends, far)
                else:
                    piece = jnp.where(lane == 0, far, near)
                lags[n, half, pl.ds(j, ROWS, stride=partners), :] = jnp.take_along_axis(piece, mirror, axis=1)

    def send(n):
        for q in range(4):
            finished(n, q).start()

    edges = [whiten_part(0)]
    form(0)
    before = None
    for n in range(len(steps)):
        pair = product(n)
        if n + 1 < len(steps):
            if steps[n + 1][0] == len(edges):
                edges.append(whiten_part(len(edges)))
            form(n + 1)
        if before is not None:
            finish(n - 1, before, edges[steps[n - 1][0]])
            send(n - 1)
        before = pair
    finish(len(steps) - 1, before, edges[-1])
    send(len(steps) - 1)
    for n in range(len(steps)):
        for q in range(4):
            finished(n, q).wait()


def correlations_of(place, own, parts, mask):
    stations = own[0].shape[0]
    partners = parts.shape[1] // 2
    vmem = pl.BlockSpec(memory_space=pltpu.VMEM)
    return pl.pallas_call(
        correlate,
        out_shape=jax.ShapeDtypeStruct((stations, SHIFTS, partners, L), jnp.float32),
        in_specs=[pl.BlockSpec(memory_space=pltpu.SMEM)] + [vmem] * 6,
        out_specs=pl.BlockSpec(memory_space=pl.ANY),
        scratch_shapes=[
            pltpu.VMEM((2, 2, partners, 16, F), jnp.bfloat16),
            pltpu.VMEM((2, 2, partners * ROWS, F), jnp.bfloat16),
            pltpu.VMEM((SHIFTS * stations // ROWS, L // 128, partners * ROWS, 128), jnp.float32),
            pltpu.SemaphoreType.DMA((SHIFTS * stations // ROWS, L // 128)),
        ],
        compiler_params=pltpu.CompilerParams(vmem_limit_bytes=24 * MIB),
        cost_estimate=pl.CostEstimate(
            flops=2 * SHIFTS * stations * partners * 2 * F * HALF,
            bytes_accessed=SHIFTS * stations * partners * L * 4,
            transcendentals=0),
    )(place, *own, parts, mask)


def shards(spectra, station_ok, pair_mask):
    bands, layers = lax.axis_size("freq"), lax.axis_size("layer")
    stations = spectra.shape[1]
    partners = stations // bands
    repeated, source = prepared(spectra, station_ok, bands)
    own = lax.all_to_all(repeated, "freq", 0, 0)
    above = lax.ppermute(source, "layer", [((i + 1) % layers, i) for i in range(layers)])
    above, own = lax.optimization_barrier((above, own))
    place = lax.axis_index("block").reshape(1)
    parts = lax.all_to_all(chosen(place, staged(source), above), ("block", "freq"), 0, 0)
    mask = pair_mask.reshape(stations, SHIFTS * partners).astype(jnp.float32) * (1.0 / math.sqrt(F))
    return correlations_of(place, whitened_block(own), parts, mask)


def solution(mesh):
    blocks, bands = mesh.shape["sta"], mesh.shape["freq"]
    inner = Mesh(mesh.devices.reshape(blocks // LAYER, LAYER, bands), ("layer", "block", "freq"))
    sta = ("layer", "block")
    return jax.shard_map(
        shards,
        mesh=inner,
        in_specs=(P(None, sta, "freq"), P(sta), P(sta, None, "freq")),
        out_specs=P(sta, None, "freq", None),
        check_vma=False,
    )
```

```python
import math

import jax
import jax.numpy as jnp
import numpy as np
import ml_dtypes
from jax import lax
from jax.experimental import pallas as pl
from jax.experimental.pallas import tpu as pltpu
from jax.sharding import Mesh, PartitionSpec as P

F = 2048
L = 512
H = 4
SHIFTS = 3
HALF = L // 2
LAYER = 4
epsilon = 1e-06
MIB = 1024 * 1024
ROWS = 32


def tables():
    bins = np.arange(F, dtype=np.int64)
    taus = np.arange(HALF, dtype=np.int64)
    angles = (bins[:, None] * taus[None, :] % (2 * F)).astype(np.float64) * (math.pi / F)
    return [half.astype(ml_dtypes.bfloat16) for half in (np.cos(angles), -np.sin(angles))]


def edge_rows():
    turn = 2 * F // HALF
    lane = lax.broadcasted_iota(jnp.int32, (8, 128), 1) % turn
    cos = sin = jnp.zeros((8, 128), jnp.float32)
    for r in range(turn):
        angle = 2 * math.pi * r / turn
        values = np.array([math.cos(angle), math.sin(angle)]).astype(ml_dtypes.bfloat16)
        cos = jnp.where(lane == r, float(values[0]), cos)
        sin = jnp.where(lane == r, float(values[1]), sin)
    return jnp.concatenate([cos] * (F // 128), axis=1), jnp.concatenate([sin] * (F // 128), axis=1)


def whitened(real, imag):
    rows = real.shape[0]
    powers = real * real + imag * imag
    total = jnp.sum(powers, axis=1, keepdims=True)
    padded = jnp.concatenate([powers, jnp.zeros((rows, 128), jnp.float32)], axis=1)
    width = padded.shape[1]
    two = padded + pltpu.roll(padded, 1, 1)
    four = two + pltpu.roll(two, 2, 1)
    eight = four + pltpu.roll(four, 4, 1)
    nine = eight + pltpu.roll(padded, 2 * H, 1)
    smooth = pltpu.roll(nine, width - H, 1)[:, :F]
    scales = lax.rsqrt(smooth * (1.0 / (2 * H + 1)) + total * (0.5 / F) + epsilon)
    return real * scales, imag * scales


def prepare(spectra_hbm, ok_hbm, repeated_ref, source_ref, spectra_ref, ok_ref, valid_ref, turned_ref, sems):
    stations = spectra_ref.shape[1]
    bands = source_ref.shape[0]
    loads = [pltpu.make_async_copy(spectra_hbm, spectra_ref, sems.at[0]), pltpu.make_async_copy(ok_hbm, ok_ref, sems.at[1])]
    for load in loads:
        load.start()
    for load in loads:
        load.wait()
    shape = (stations, stations)
    here = lax.broadcasted_iota(jnp.int32, shape, 0) == lax.broadcasted_iota(jnp.int32, shape, 1)
    ok = jnp.where(here, jnp.broadcast_to(ok_ref[...].astype(jnp.float32), shape), 0.0)
    ok = jnp.sum(ok, axis=1, keepdims=True)
    real = spectra_ref[0].astype(jnp.float32) * ok
    imag = spectra_ref[1].astype(jnp.float32) * ok
    valid_ref[0] = real.astype(jnp.bfloat16)
    valid_ref[1] = imag.astype(jnp.bfloat16)
    stores = [pltpu.make_async_copy(valid_ref, repeated_ref.at[q], sems.at[2 + q]) for q in range(bands)]
    for store in stores:
        store.start()
    turn(real, imag, turned_ref)
    stores.append(pltpu.make_async_copy(turned_ref, source_ref, sems.at[2 + bands]))
    stores[-1].start()
    for store in stores:
        store.wait()


def prepared(spectra, station_ok, bands):
    _, stations, bins = spectra.shape
    turned = (bands, 2 * stations // bands, bins)
    hbm = pl.BlockSpec(memory_space=pl.ANY)
    return pl.pallas_call(
        prepare,
        out_shape=[jax.ShapeDtypeStruct((bands,) + spectra.shape, spectra.dtype),
                   jax.ShapeDtypeStruct(turned, spectra.dtype)],
        in_specs=[hbm] * 2,
        out_specs=[hbm] * 2,
        scratch_shapes=[
            pltpu.VMEM(spectra.shape, spectra.dtype),
            pltpu.VMEM((1, stations), jnp.int32),
            pltpu.VMEM(spectra.shape, spectra.dtype),
            pltpu.VMEM(turned, spectra.dtype),
            pltpu.SemaphoreType.DMA((3 + bands,)),
        ],
        compiler_params=pltpu.CompilerParams(vmem_limit_bytes=60 * MIB),
        cost_estimate=pl.CostEstimate(flops=spectra.size, bytes_accessed=2 * 10 * spectra.size, transcendentals=0),
    )(spectra, station_ok.reshape(1, stations))


def turn(real, imag, turned_ref):
    bands, both_rows, _ = turned_ref.shape
    partners = both_rows // 2
    for q in range(bands):
        rows = slice(q * partners, (q + 1) * partners)
        turned_ref[q] = jnp.concatenate([real[rows], imag[rows]], axis=0).astype(jnp.bfloat16)


def stage(source_ref, staged_ref):
    staged_ref[...] = source_ref[...]


def staged(source):
    vmem = pl.BlockSpec(memory_space=pltpu.VMEM)
    return pl.pallas_call(
        stage,
        out_shape=jax.ShapeDtypeStruct(source.shape, source.dtype),
        in_specs=[vmem],
        out_specs=vmem,
        compiler_params=pltpu.CompilerParams(vmem_limit_bytes=8 * MIB),
        cost_estimate=pl.CostEstimate(flops=0, bytes_accessed=4 * source.size, transcendentals=0),
    )(source)


def choose(place_ref, source_ref, above_ref, sent_ref, sems):
    bands = source_ref.shape[0]

    def copy(other, ref):
        return pltpu.make_async_copy(ref, sent_ref.at[pl.ds(other * bands, bands)], sems.at[other])

    for other in range(LAYER):
        pl.when(other < place_ref[0])(lambda: copy(other, source_ref).start())
        pl.when(other >= place_ref[0])(lambda: copy(other, above_ref).start())
    for other in range(LAYER):
        copy(other, source_ref).wait()


def chosen(place, source, above):
    vmem = pl.BlockSpec(memory_space=pltpu.VMEM)
    return pl.pallas_call(
        choose,
        out_shape=jax.ShapeDtypeStruct((LAYER * source.shape[0],) + source.shape[1:], source.dtype),
        in_specs=[pl.BlockSpec(memory_space=pltpu.SMEM)] + [vmem] * 2,
        out_specs=pl.BlockSpec(memory_space=pl.ANY),
        scratch_shapes=[pltpu.SemaphoreType.DMA((LAYER,))],
        compiler_params=pltpu.CompilerParams(vmem_limit_bytes=8 * MIB),
        cost_estimate=pl.CostEstimate(flops=0, bytes_accessed=2 * 6 * source.size, transcendentals=0),
    )(place, source, above)


def whiten(own_ref, cos_from, sin_from, real_ref, imag_ref, cos_ref, sin_ref, sems):
    bands = own_ref.shape[0]
    pairs = ((cos_from, cos_ref), (sin_from, sin_ref))
    loads = [pltpu.make_async_copy(table, to, sems.at[i]) for i, (table, to) in enumerate(pairs)]
    for load in loads:
        load.start()

    def some(group, carry):
        at = pl.ds(pl.multiple_of(group * 16, 16), 16)
        real = jnp.concatenate([own_ref[q, 0, at, :] for q in range(bands)], axis=1)
        imag = jnp.concatenate([own_ref[q, 1, at, :] for q in range(bands)], axis=1)
        real, imag = whitened(real.astype(jnp.float32), imag.astype(jnp.float32))
        real_ref[at, :] = real.astype(jnp.bfloat16)
        imag_ref[at, :] = imag.astype(jnp.bfloat16)
        return carry

    lax.fori_loop(0, real_ref.shape[0] // 16, some, 0)
    for load in loads:
        load.wait()


def whitened_block(own):
    stations = own.shape[2]
    given = [jnp.asarray(table) for table in tables()]
    vmem = pl.BlockSpec(memory_space=pltpu.VMEM)
    return pl.pallas_call(
        whiten,
        out_shape=[jax.ShapeDtypeStruct((stations, F), jnp.bfloat16)] * 2
        + [jax.ShapeDtypeStruct(table.shape, table.dtype) for table in given],
        in_specs=[vmem] + [pl.BlockSpec(memory_space=pl.ANY)] * 2,
        out_specs=[vmem] * 4,
        scratch_shapes=[pltpu.SemaphoreType.DMA((2,))],
        compiler_params=pltpu.CompilerParams(vmem_limit_bytes=8 * MIB),
        cost_estimate=pl.CostEstimate(flops=30 * stations * F, bytes_accessed=8 * stations * F, transcendentals=stations * F),
    )(own, *given)


def correlate(place_ref, own_real, own_imag, cos_ref, sin_ref, part_ref, mask_ref, out_ref,
              others, cross, lags, sems):
    stations = own_real.shape[0]
    bands = part_ref.shape[0] // LAYER
    partners = part_ref.shape[1] // 2
    last_cos, last_sin = edge_rows()
    lane = lax.broadcasted_iota(jnp.int32, (ROWS, 128), 1)
    mirror = lax.rem(128 - lane, 128)
    steps = [(k, slice(i, i + ROWS)) for k in range(SHIFTS) for i in range(0, stations, ROWS)]

    def whiten_part(k):
        first = lax.rem(place_ref[0] + (k + 1), LAYER) * bands
        both = jnp.concatenate([part_ref[first + q] for q in range(bands)], axis=1).astype(jnp.float32)
        real, imag = whitened(both[:partners], both[partners:])
        real = real.astype(jnp.bfloat16).astype(jnp.float32)
        imag = imag.astype(jnp.bfloat16).astype(jnp.float32)
        for j in range(partners):
            others[k % 2, 0, j] = jnp.broadcast_to(real[j:j + 1], (16, F)).astype(jnp.bfloat16)
            others[k % 2, 1, j] = jnp.broadcast_to(imag[j:j + 1], (16, F)).astype(jnp.bfloat16)
        edge = jnp.zeros((stations, partners), jnp.float32)
        for own, turned in ((own_real, real * last_cos - imag * last_sin), (own_imag, imag * last_cos + real * last_sin)):
            edge = edge + lax.dot_general(own[...], turned.astype(jnp.bfloat16), (((1,), (1,)), ((), ())),
                                          preferred_element_type=jnp.float32)
        return edge * mask_ref[:, k * partners:(k + 1) * partners]

    def form(n):
        k, rows = steps[n]
        for j in range(partners):
            for i in range(0, ROWS, 16):
                real = own_real[rows.start + i:rows.start + i + 16, :]
                imag = own_imag[rows.start + i:rows.start + i + 16, :]
                other_real, other_imag = others[k % 2, 0, j], others[k % 2, 1, j]
                at = slice(j * ROWS + i, j * ROWS + i + 16)
                cross[n % 2, 0, at, :] = real * other_real + imag * other_imag
                cross[n % 2, 1, at, :] = imag * other_real - real * other_imag

    def product(n):
        return (jnp.dot(cross[n % 2, 0], cos_ref[...], preferred_element_type=jnp.float32),
                jnp.dot(cross[n % 2, 1], sin_ref[...], preferred_element_type=jnp.float32))

    def finished(n, q):
        k, rows = steps[n]
        ready = lags.at[n, q].reshape(ROWS, partners, 128)
        return pltpu.make_async_copy(ready, out_ref.at[pl.ds(rows.start, ROWS), k, :, pl.ds(q * 128, 128)], sems.at[n, q])

    def finish(n, pair, edge):
        k, rows = steps[n]
        even, odd = pair
        down = []
        for half in (0, 1):
            for j in range(partners):
                weight = mask_ref[rows, k * partners + j:k * partners + j + 1]
                at = slice(j * ROWS, (j + 1) * ROWS)
                c = even[at, half * 128:(half + 1) * 128] * weight
                s = odd[at, half * 128:(half + 1) * 128] * weight
                lags[n, 2 + half, pl.ds(j, ROWS, stride=partners), :] = c + s
                down.append(c - s)
        for half in (0, 1):
            for j in range(partners):
                near, far = down[j], down[partners + j]
                if half == 0:
                    ends = jnp.broadcast_to(edge[rows, j:j + 1], (ROWS, 128))
                    piece = jnp.where(lane == 0, ends, far)
                else:
                    piece = jnp.where(lane == 0, far, near)
                lags[n, half, pl.ds(j, ROWS, stride=partners), :] = jnp.take_along_axis(piece, mirror, axis=1)

    def send(n):
        for q in range(4):
            finished(n, q).start()

    edges = [whiten_part(0)]
    form(0)
    before = None
    for n in range(len(steps)):
        if n + 1 < len(steps):
            if steps[n + 1][0] == len(edges):
                edges.append(whiten_part(len(edges)))
            form(n + 1)
        pair = product(n)
        if before is not None:
            finish(n - 1, before, edges[steps[n - 1][0]])
            send(n - 1)
        before = pair
    finish(len(steps) - 1, before, edges[-1])
    send(len(steps) - 1)
    for n in range(len(steps)):
        for q in range(4):
            finished(n, q).wait()


def correlations_of(place, own, parts, mask):
    stations = own[0].shape[0]
    partners = parts.shape[1] // 2
    vmem = pl.BlockSpec(memory_space=pltpu.VMEM)
    return pl.pallas_call(
        correlate,
        out_shape=jax.ShapeDtypeStruct((stations, SHIFTS, partners, L), jnp.float32),
        in_specs=[pl.BlockSpec(memory_space=pltpu.SMEM)] + [vmem] * 6,
        out_specs=pl.BlockSpec(memory_space=pl.ANY),
        scratch_shapes=[
            pltpu.VMEM((2, 2, partners, 16, F), jnp.bfloat16),
            pltpu.VMEM((2, 2, partners * ROWS, F), jnp.bfloat16),
            pltpu.VMEM((SHIFTS * stations // ROWS, L // 128, partners * ROWS, 128), jnp.float32),
            pltpu.SemaphoreType.DMA((SHIFTS * stations // ROWS, L // 128)),
        ],
        compiler_params=pltpu.CompilerParams(vmem_limit_bytes=24 * MIB),
        cost_estimate=pl.CostEstimate(
            flops=2 * SHIFTS * stations * partners * 2 * F * HALF,
            bytes_accessed=SHIFTS * stations * partners * L * 4,
            transcendentals=0),
    )(place, *own, parts, mask)


def shards(spectra, station_ok, pair_mask):
    bands, layers = lax.axis_size("freq"), lax.axis_size("layer")
    stations = spectra.shape[1]
    partners = stations // bands
    repeated, source = prepared(spectra, station_ok, bands)
    own = lax.all_to_all(repeated, "freq", 0, 0)
    above = lax.ppermute(source, "layer", [((i + 1) % layers, i) for i in range(layers)])
    above, own = lax.optimization_barrier((above, own))
    place = lax.axis_index("block").reshape(1)
    parts = lax.all_to_all(chosen(place, staged(source), above), ("block", "freq"), 0, 0)
    mask = pair_mask.reshape(stations, SHIFTS * partners).astype(jnp.float32) * (1.0 / math.sqrt(F))
    return correlations_of(place, whitened_block(own), parts, mask)


def solution(mesh):
    blocks, bands = mesh.shape["sta"], mesh.shape["freq"]
    inner = Mesh(mesh.devices.reshape(blocks // LAYER, LAYER, bands), ("layer", "block", "freq"))
    sta = ("layer", "block")
    return jax.shard_map(
        shards,
        mesh=inner,
        in_specs=(P(None, sta, "freq"), P(sta), P(sta, None, "freq")),
        out_specs=P(sta, None, "freq", None),
        check_vma=False,
    )
```
